128 devices in a mesh: col: 32 (over x_hi, z, y), row: 4 (over x_lo, core).
Axes of the slice: x: 4 (x_hi: 2, x_lo: 2; x = x_hi * 2 + x_lo), y: 4, z: 4, core: 2. Of those that a mesh axis runs over, the one named last changes fastest.
Arguments:
- sigma_anc: float32 [64, 64, 128, 128], P('row', 'col'), as said below
- panel_u: float32 [32, 32, 128, 128], P('col'), may hold values from -0.09375 to 0.09375
- structure: int32 [32, 32], P('col'), may hold values from 0 to 63, as said below
- diag_inv: float32 [32, 128, 128], P('col'), may hold values from -0.5 to 0.5
Outputs:
- panel_out: float32 [32, 64, 128, 128], P('col', 'row')
- diag_out: float32 [32, 128, 128], P('col')
The draws below stay inside these ranges and needn't reach their ends.
Inputs may be any that keep to these rules, and one draw needn't show every extreme that they name: `structure`: each row holds 32 different ancestor numbers in increasing order. `sigma_anc`: the matrix is symmetric: block (a, b) is the transpose of block (b, a).
All inputs are finite; a program needn't handle non-finite values.
Results may differ from the reference program's by a relative error of at most 0.0003.
Values sent between devices are 32-bit elements; how exact they have to be, the bound alone decides.
No kernel may reach another device: no remote copies, remote signals or barrier semaphores. Data moves between devices by JAX's collectives and lax.ppermute only.
A program may use at most 128 MiB of HBM per device.

```python
import jax
import jax.numpy as jnp
from jax import lax

B = 128
NA = 64
K = 32
NS = 32


def draw_sigma_anc(key, part):
    side = NA * B
    base = jax.random.normal(jax.random.fold_in(key, 11), (side, side), jnp.float32)
    full = (base + base.T) * 0.7
    return full.reshape(NA, B, NA, B).transpose(0, 2, 1, 3)


def draw_structure(key, part):
    keys = jax.random.split(jax.random.fold_in(key, 17), NS)
    perms = jax.vmap(lambda k: jax.random.permutation(k, NA))(keys).astype(jnp.int32)
    chosen = perms[:, :K]
    inner = 1 + jax.random.permutation(jax.random.fold_in(key, 19), NA - 2)[:K - 2].astype(jnp.int32)
    first = jnp.concatenate([jnp.array([0, NA - 1], jnp.int32), inner])
    chosen = chosen.at[0].set(first)
    return jnp.sort(chosen, axis=1).astype(jnp.int32)


def block_levels(rng, dims, shards, low, high):
    gain, own = 1.0, jax.random.fold_in(rng, 6)
    for axis_at, blocks in shards:
        steps = jnp.exp(jax.random.uniform(jax.random.fold_in(own, axis_at), (blocks,), jnp.float32, low / len(shards), high / len(shards)))
        gain = gain * jnp.repeat(steps, dims[axis_at] // blocks).reshape([-1 if axis == axis_at else 1 for axis in range(len(dims))])
    return gain


def centred(key, shape, width, most, cuts=(), kind=jnp.bfloat16):
    level = block_levels(key, shape, cuts, -0.22, 0.18) if cuts else 1.0
    drawn = jax.random.normal(key, shape, jnp.float32) * width * level
    return jnp.minimum(jnp.maximum(drawn, -most), most).astype(kind)


def setup_inputs(seed: int = 0) -> dict:
    key_of = jax.random.split(jax.random.key(seed), 5)
    sigma_anc = draw_sigma_anc(jax.random.fold_in(key_of[4], 71), 0)
    panel_u = centred(key_of[1], (NS, K, B, B), (K * B) ** -0.5, 0.09375, ((0, 32),), jnp.float32)
    structure = draw_structure(jax.random.fold_in(key_of[4], 71), 0)
    diag_inv = centred(key_of[3], (NS, B, B), B ** -0.5, 0.5, ((0, 32),), jnp.float32)
    return dict(sigma_anc=sigma_anc, panel_u=panel_u, structure=structure, diag_inv=diag_inv)


def reference(sigma_anc, panel_u, structure, diag_inv):
    whole = sigma_anc.transpose(0, 2, 1, 3).reshape(NA * B, NA * B)
    offsets = jnp.arange(B, dtype=jnp.int32)
    ancestors = jnp.arange(NA, dtype=jnp.int32)

    def one_node(items):
        blocks, picks, inverse = items
        columns = (picks[:, None] * B + offsets[None, :]).reshape(-1).astype(jnp.int32)
        chosen = jnp.take(whole, columns, axis=1)
        stacked = blocks.reshape(K * B, B)
        result = jnp.dot(chosen, stacked, precision=lax.Precision.HIGHEST, preferred_element_type=jnp.float32)
        member = jnp.any(picks[None, :] == ancestors[:, None], axis=1).astype(jnp.float32)
        panel = -result.reshape(NA, B, B) * member[:, None, None]
        onehot = (picks[:, None] == ancestors[None, :]).astype(jnp.float32)
        dense = jnp.einsum("ka,kxy->axy", onehot, blocks, precision=lax.Precision.HIGHEST)
        update = jnp.dot(dense.reshape(NA * B, B).T, panel.reshape(NA * B, B), precision=lax.Precision.HIGHEST, preferred_element_type=jnp.float32)
        base = jnp.dot(inverse.T, inverse, precision=lax.Precision.HIGHEST, preferred_element_type=jnp.float32)
        return panel, base - update

    panel_out, diag_out = lax.map(one_node, (panel_u, structure, diag_inv))
    return panel_out, diag_out
```

```python
import functools

import jax
import jax.numpy as jnp
from jax import lax
from jax.experimental import pallas as pl
from jax.experimental.pallas import tpu as pltpu
from jax.sharding import PartitionSpec as P

AXES = ("col", "row")
CORE = 1
X1, X3 = 2, 66
Y1, Y2, Y3 = 4, 8, 12
Z1, Z2, Z3 = 16, 32, 48
B = 128
Q = 32
F32, BF16 = jnp.float32, jnp.bfloat16


def swap(x, mask):
    return lax.ppermute(x, AXES, [(i, i ^ mask) for i in range(128)])


def split(x):
    hi = x.astype(BF16)
    return hi, (x - hi.astype(F32)).astype(BF16)


def dot(a, b):
    return jnp.dot(a, b, preferred_element_type=F32)


def dot3(a, b):
    (ah, al), (bh, bl) = split(a), split(b)
    return dot(ah, bh) + (dot(ah, bl) + dot(al, bh))


def cut_kernel(where, u_ref, label_ref, first_ref, second_ref, turned):
    half = u_ref.shape[0] // 2

    def step(k, carry):
        for i, out_ref in enumerate((first_ref, second_ref)):
            turned[i] = u_ref[i * half + k].T
            out_ref[k] = turned[i, pl.ds(pl.multiple_of(where[0] * Q, Q), Q), :]
        return carry

    lax.fori_loop(0, half, step, 0)
    first_ref[half] = jnp.broadcast_to(label_ref[...].astype(F32), (Q, B))


def cut(panel, labels, row):
    return pl.pallas_call(
        cut_kernel,
        grid_spec=pltpu.PrefetchScalarGridSpec(
            num_scalar_prefetch=1,
            grid=(1,),
            in_specs=[
                pl.BlockSpec((32, B, B), lambda i, w: (0, 0, 0)),
                pl.BlockSpec((1, B), lambda i, w: (0, 0)),
            ],
            out_specs=[pl.BlockSpec((n, Q, B), lambda i, w: (0, 0, 0)) for n in (17, 16)],
            scratch_shapes=[pltpu.VMEM((2, B, B), F32)],
        ),
        out_shape=[jax.ShapeDtypeStruct((n, Q, B), F32) for n in (17, 16)],
        name="cut",
    )(row[None], panel, labels)


def spread_kernel(table, w_ref, hi_ref, lo_ref):
    first = pl.program_id(0) * hi_ref.shape[0]
    for i in range(hi_ref.shape[0]):
        for q in range(16):
            at = table[q * 64 + first + i]
            part = w_ref[jnp.maximum(at, 0)]
            part = jnp.where(at >= 0, part, 0.0)
            hi, lo = split(part)
            hi_ref[i, q * Q : (q + 1) * Q, :] = hi
            lo_ref[i, q * Q : (q + 1) * Q, :] = lo


def spread(table, pieces):
    step = 4
    block = pl.BlockSpec((step, 16 * Q, B), lambda i, t: (i, 0, 0))
    return pl.pallas_call(
        spread_kernel,
        grid_spec=pltpu.PrefetchScalarGridSpec(
            num_scalar_prefetch=1,
            grid=(64 // step,),
            in_specs=[pl.BlockSpec((528, Q, B), lambda i, t: (0, 0, 0))],
            out_specs=[block, block],
        ),
        out_shape=[jax.ShapeDtypeStruct((64, 16 * Q, B), BF16)] * 2,
        compiler_params=pltpu.CompilerParams(vmem_limit_bytes=40 << 20),
        cost_estimate=pl.CostEstimate(flops=1 << 22, bytes_accessed=24 << 20, transcendentals=0),
        name="spread",
    )(table, pieces)


def product_kernel(has_start, where, *refs):
    hi0, hi1, lo0, lo1, left0, left1, right0, right1 = refs[:8]
    out_ref, total = refs[-2:]
    step = pl.program_id(0)
    own = where[2]

    @pl.when(step == 0)
    def _():
        if has_start:
            total[:, :B] = refs[8][own]
            total[:, B:] = refs[8][1 - own]
        else:
            total[...] = jnp.zeros_like(total)

    sigma = jnp.concatenate(
        [
            jnp.concatenate([left0[0], right0[0]], axis=1),
            jnp.concatenate([left1[0], right1[0]], axis=1),
        ],
        axis=0,
    )
    high, low = split(sigma)
    wh = jnp.concatenate([hi0[0], hi1[0]], axis=1)
    wl = jnp.concatenate([lo0[0], lo1[0]], axis=1)
    total[...] += dot(wh, high) + (dot(wh, low) + dot(wl, high))

    @pl.when(step == pl.num_programs(0) - 1)
    def _():
        out_ref[own] = total[:, :B]
        out_ref[1 - own] = total[:, B:]


def product(where, hi, lo, left, right, start=None):
    rows = 16 * Q
    w0 = pl.BlockSpec((1, rows, B), lambda i, w: (w[0] + i, 0, 0))
    w1 = pl.BlockSpec((1, rows, B), lambda i, w: (w[1] + i, 0, 0))
    s = pl.BlockSpec((1, B, B), lambda i, w: (i, 0, 0))
    whole = pl.BlockSpec((2, rows, B), lambda i, w: (0, 0, 0))
    more = [] if start is None else [start]
    return pl.pallas_call(
        functools.partial(product_kernel, start is not None),
        grid_spec=pltpu.PrefetchScalarGridSpec(
            num_scalar_prefetch=1,
            grid=(16,),
            in_specs=[w0, w1, w0, w1, s, s, s, s] + [whole] * len(more),
            out_specs=whole,
            scratch_shapes=[pltpu.VMEM((rows, 2 * B), F32)],
        ),
        out_shape=jax.ShapeDtypeStruct((2, rows, B), F32),
        compiler_params=pltpu.CompilerParams(vmem_limit_bytes=40 << 20),
        cost_estimate=pl.CostEstimate(flops=6 * 512 * 4096 * 256, bytes_accessed=14 << 20, transcendentals=0),
        name="product",
    )(where, hi, hi, lo, lo, *left, *right, *more)


def finish_kernel(where, picks, u_ref, keep0, come0, keep1, come1, panel_ref, share_ref, total):
    even = where[0] == 0
    total[...] = jnp.zeros_like(total)
    for t in range(8):
        for low, (keep, come) in enumerate(((keep0, come0), (keep1, come1))):
            a = 2 * t + low
            pick = picks[a]
            parts = []
            for x in range(2):
                k, c = keep[x, t], come[x, t]
                parts += [jnp.where(even, k, c), jnp.where(even, c, k)]
            turned = jnp.concatenate(parts, axis=0)
            panel_ref[a] = jnp.where(pick >= 0, -turned.T, 0.0)

            @pl.when(pick >= 0)
            def _(turned=turned, pick=pick):
                total[...] += dot3(turned, u_ref[jnp.maximum(pick, 0)])

    share_ref[...] = total[...].T


def finish(core, picks, panel, parts):
    full = lambda *s: pl.BlockSpec(s, lambda i, w, p: (0,) * len(s))
    return pl.pallas_call(
        finish_kernel,
        grid_spec=pltpu.PrefetchScalarGridSpec(
            num_scalar_prefetch=2,
            grid=(1,),
            in_specs=[full(32, B, B)] + [full(2, 8, Q, B)] * 4,
            out_specs=[full(16, B, B), full(B, B)],
            scratch_shapes=[pltpu.VMEM((B, B), F32)],
        ),
        out_shape=[jax.ShapeDtypeStruct((16, B, B), F32), jax.ShapeDtypeStruct((B, B), F32)],
        compiler_params=pltpu.CompilerParams(vmem_limit_bytes=40 << 20),
        name="finish",
    )(core[None], picks, panel, *parts)


def gather_w(first, second):
    a = jnp.stack([first, swap(first, Z1), swap(first, Z2), swap(first, Z3)])
    b = jnp.stack([second, swap(second, Y1), swap(second, Y2), swap(second, Y3)])
    a1, a3 = swap(a, Y1), swap(a, Y3)
    b1, b3 = swap(b, Z1), swap(b, Z3)
    a2 = [swap(a3[:2], Y1), swap(a1[2:], Y3)]
    b2 = [swap(b3[:2], Z1), swap(b1[2:], Z3)]
    parts = [t.reshape(-1, Q, B) for t in (a, a1, *a2, a3, b, b1, *b2, b3)]
    return jnp.concatenate(parts)


def gather_sigma(s):
    x1, x3 = swap(s, X1), swap(s, X3)
    x2 = jnp.concatenate([swap(x3[:8], X1), swap(x1[8:], X3)])
    return [(t, swap(t, CORE)) for t in (s, x1, x3, x2)]


def local(sigma_anc, panel_u, structure, diag_inv):
    col, row = lax.axis_index("col"), lax.axis_index("row")
    x_hi, z, y = col // 16, (col // 4) % 4, col % 4
    x_lo, core = row // 2, row % 2
    panel = panel_u[0]

    gathered = [gather_sigma(sigma_anc[:, i]) for i in range(2)]
    labels = jnp.pad(structure, ((0, 0), (0, B - 32)))
    pieces = gather_w(*cut(panel, labels, row))

    node = jnp.arange(16, dtype=jnp.int32)
    dz, dy = (node // 4) ^ z, (node % 4) ^ y
    there = pieces[: 16 * 17].reshape(16, 17, Q, B)[:, 16, 0, :32].astype(jnp.int32)
    chosen = jnp.sum(jnp.where((dy * 4 + dz)[:, None, None] == node[None, :, None], there[None], 0), axis=1)
    ancestors = jnp.arange(64, dtype=jnp.int32)
    entry = jnp.arange(32, dtype=jnp.int32)
    pick = jnp.sum(jnp.where(chosen[:, :, None] == ancestors, entry[None, :, None] + 1, 0), axis=1) - 1
    first = ((dy * 4 + dz) * 17)[:, None] + pick
    second = (16 * 17 + (dz * 4 + dy) * 16)[:, None] + pick - 16
    table = jnp.where(pick < 0, -1, jnp.where(pick < 16, first, second)).reshape(-1)
    mine = jnp.sum(jnp.where(structure[0][:, None] == (16 * row + jnp.arange(16))[None, :], entry[:, None] + 1, 0), axis=0) - 1

    hi, lo = spread(table, pieces)
    own = jnp.stack([32 * x_lo + 16 * core, 32 * x_lo + 16 * (1 - core), x_hi])
    other = jnp.stack([32 * (1 - x_lo) + 16 * core, 32 * (1 - x_lo) + 16 * (1 - core), x_hi])
    groups = [
        [h * 64 + q * 4 + l * 2 + c for l in range(2) for q in range(16)] for h in range(2) for c in range(2)
    ]
    parts = []
    for s, x1, x3, x2 in gathered:
        part = product(other, hi, lo, x1, x3)
        part = product(own, hi, lo, s, x2, part)
        moved = lax.all_to_all(part.reshape(32, Q, B), AXES, 0, 0, axis_index_groups=groups, tiled=True)
        moved = moved.reshape(2, 2, 8, Q, B)
        keep = lax.dynamic_index_in_dim(moved, core, 1, keepdims=False)
        send = lax.dynamic_index_in_dim(moved, 1 - core, 1, keepdims=False)
        parts += [keep, swap(send, CORE)]

    panel_out, share = finish(core, mine, panel, parts)
    base = jnp.einsum("zx,zy->xy", diag_inv[0], diag_inv[0], precision=lax.Precision.HIGHEST)
    diag = base + jnp.sum(lax.all_gather(share, "row"), axis=0)
    return panel_out[None], diag[None]


def solution(mesh):
    return jax.shard_map(
        local,
        mesh=mesh,
        in_specs=(P("row", "col", None, None), P("col", None, None, None), P("col", None), P("col", None, None)),
        out_specs=(P("col", "row", None, None), P("col", None, None)),
        check_vma=False,
    )
```

```python
import functools

import jax
import jax.numpy as jnp
from jax import lax
from jax.experimental import pallas as pl
from jax.experimental.pallas import tpu as pltpu
from jax.sharding import PartitionSpec as P

AXES = ("col", "row")
CORE = 1
X1, X3 = 2, 66
Y1, Y3 = 4, 12
Z1, Z3 = 16, 48
B = 128
Q = 32
F32, BF16 = jnp.float32, jnp.bfloat16
MANY = 4


def swap(x, even, odd=None):
    odd = even if odd is None else odd
    return lax.ppermute(x, AXES, [(i, i ^ (odd if i % 2 else even)) for i in range(128)])


def ring(x, one, three):
    first = swap(x, one, three)
    second = swap(x, three, one)
    return first, second, swap(second, one, three)


def split(x):
    hi = x.astype(BF16)
    return hi, (x - hi.astype(F32)).astype(BF16)


def dot(a, b):
    return jnp.dot(a, b, preferred_element_type=F32)


def dot3(a, b):
    (ah, al), (bh, bl) = split(a), split(b)
    return dot(ah, bh) + (dot(ah, bl) + dot(al, bh))


def cut_kernel(where, u_ref, label_ref, first_ref, second_ref, turned):
    half = u_ref.shape[0] // 2

    def step(k, carry):
        for i, out_ref in enumerate((first_ref, second_ref)):
            turned[i] = u_ref[i * half + k].T
            out_ref[k] = turned[i, pl.ds(pl.multiple_of(where[0] * Q, Q), Q), :]
        return carry

    lax.fori_loop(0, half, step, 0, unroll=4)
    for out_ref in (first_ref, second_ref):
        out_ref[half] = jnp.zeros_like(out_ref[half])
        out_ref[half, :, :32] = jnp.broadcast_to(label_ref[...].astype(F32), (Q, 32))


def cut(panel, labels, row):
    return pl.pallas_call(
        cut_kernel,
        grid_spec=pltpu.PrefetchScalarGridSpec(
            num_scalar_prefetch=1,
            grid=(1,),
            in_specs=[
                pl.BlockSpec((32, B, B), lambda i, w: (0, 0, 0)),
                pl.BlockSpec((1, 32), lambda i, w: (0, 0)),
            ],
            out_specs=[pl.BlockSpec((17, Q, B), lambda i, w: (0, 0, 0))] * 2,
            scratch_shapes=[pltpu.VMEM((2, B, B), F32)],
        ),
        out_shape=[jax.ShapeDtypeStruct((17, Q, B), F32)] * 2,
        name="cut",
    )(row[None], panel, labels)


ON_CHIP = pl.BlockSpec(memory_space=pltpu.VMEM)
SCALARS = pl.BlockSpec(memory_space=pltpu.SMEM)


def gained(weights, blocks, sides):
    tall = [
        jnp.concatenate([blocks[side][core][i, low] for side in range(sides) for low in range(2)], axis=1)
        for core in range(2)
        for i in range(MANY)
    ]
    high, low = split(jnp.concatenate(tall, axis=0))
    wh, wl = (jnp.concatenate(t, axis=1) for t in weights)
    return dot(wh, high) + (dot(wh, low) + dot(wl, high))


def first_kernel(nodes, where, *refs):
    parts, sigmas = refs[:8], refs[8:14]
    out_ref, hi_out, lo_out, hi_ref, lo_ref, held, total, labels, arrived, left, read = refs[14:]
    texts = [
        pltpu.make_async_copy(t.at[:, 16, pl.ds(0, 8)], labels.at[i], read.at[i]) for i, t in enumerate(parts)
    ]
    for copy in texts:
        copy.start()
    copies = [pltpu.make_async_copy(t, held.at[i], arrived.at[i]) for i, t in enumerate(sigmas)]
    for copy in copies:
        copy.start()

    def clear(b, carry):
        hi_ref[b] = jnp.zeros_like(hi_ref[b])
        lo_ref[b] = jnp.zeros_like(lo_ref[b])
        return carry

    lax.fori_loop(0, hi_ref.shape[0], clear, 0)
    for copy in texts:
        copy.wait()
    for i, part in enumerate(parts):
        def node(n, carry, i=i, part=part):
            rows = pl.ds(pl.multiple_of(nodes[i * 4 + n] * Q, Q), Q)
            for k in range(16):
                at = labels[i, n, 0, i // 4 * 16 + k].astype(jnp.int32)
                hi, lo = split(part[n, k])
                hi_ref[at, rows, :] = hi
                lo_ref[at, rows, :] = lo
            return carry

        lax.fori_loop(0, 4, node, 0)

    outward = [
        pltpu.make_async_copy(ref.at[pl.ds(where[2 + core], 16)], out.at[pl.ds(16 * core, 16)], left.at[2 * i + core])
        for i, (ref, out) in enumerate(((hi_ref, hi_out), (lo_ref, lo_out)))
        for core in range(2)
    ]
    for copy in outward:
        copy.start()
    for copy in copies:
        copy.wait()

    def run(first, sides, blocks):
        def step(t, carry):
            k = pl.multiple_of(t * MANY, MANY)
            weights = [
                [ref[where[first + core] + k + i] for core in range(2) for i in range(MANY)] for ref in (hi_ref, lo_ref)
            ]
            here = [[held.at[i, pl.ds(k, MANY)] for i in side] for side in blocks]
            total[:, : 2 * sides * B] += gained(weights, here, sides)
            return carry

        lax.fori_loop(0, 16 // MANY, step, 0)

    total[...] = jnp.zeros_like(total)
    run(0, 2, [(0, 1), (2, 3)])
    at = where[4]
    for n in range(4):
        out_ref[at ^ (n // 2), :, n % 2] = total[:, n * B : (n + 1) * B].reshape(16, Q, B)
    total[...] = jnp.zeros_like(total)
    run(2, 1, [(4, 5)])
    for n in range(2):
        out_ref[where[5], :, n] += total[:, n * B : (n + 1) * B].reshape(16, Q, B)
    for copy in outward:
        copy.wait()


def first_sums(nodes, where, parts, sigmas):
    whole = pl.BlockSpec(memory_space=pl.ANY)
    rows = 16 * Q
    return pl.pallas_call(
        first_kernel,
        in_specs=[SCALARS] * 2 + [ON_CHIP] * 8 + [whole] * 6,
        out_specs=[ON_CHIP, whole, whole],
        out_shape=[jax.ShapeDtypeStruct((2, 16, 2, Q, B), F32)] + [jax.ShapeDtypeStruct((32, rows, B), BF16)] * 2,
        scratch_shapes=[
            pltpu.VMEM((64, rows, B), BF16),
            pltpu.VMEM((64, rows, B), BF16),
            pltpu.VMEM((6, 16, 2, B, B), F32),
            pltpu.VMEM((rows, 4 * B), F32),
            pltpu.SMEM((8, 4, 8, B), F32),
            pltpu.SemaphoreType.DMA((6,)),
            pltpu.SemaphoreType.DMA((4,)),
            pltpu.SemaphoreType.DMA((8,)),
        ],
        compiler_params=pltpu.CompilerParams(vmem_limit_bytes=38 << 20),
        cost_estimate=pl.CostEstimate(flops=9 << 31, bytes_accessed=32 << 20, transcendentals=0),
        name="first_sums",
    )(nodes, where, *parts, *sigmas)


def last_kernel(where, hi0, hi1, lo0, lo1, far0, far1, start, out_ref, total):
    step, at = pl.program_id(0), where[0]

    @pl.when(step == 0)
    def _():
        for n in range(2):
            total[:, n * B : (n + 1) * B] = start[at, :, n].reshape(16 * Q, B)

    weights = [[t[i] for t in pair for i in range(MANY)] for pair in ((hi0, hi1), (lo0, lo1))]
    total[...] += gained(weights, [(far0, far1)], 1)

    @pl.when(step == pl.num_programs(0) - 1)
    def _():
        for n in range(2):
            out_ref[at, :, n] = total[:, n * B : (n + 1) * B].reshape(16, Q, B)
        out_ref[1 - at] = start[1 - at]


def last_sums(at, hi, lo, far, start):
    rows = 16 * Q
    w = [pl.BlockSpec((MANY, rows, B), lambda i, w, core=core: (core * (16 // MANY) + i, 0, 0)) for core in range(2)]
    s = pl.BlockSpec((MANY, 2, B, B), lambda i, w: (i, 0, 0, 0))
    whole = pl.BlockSpec(start.shape, lambda i, w: (0,) * 5)
    return pl.pallas_call(
        last_kernel,
        grid_spec=pltpu.PrefetchScalarGridSpec(
            num_scalar_prefetch=1,
            grid=(16 // MANY,),
            in_specs=w + w + [s, s, whole],
            out_specs=whole,
            scratch_shapes=[pltpu.VMEM((rows, 2 * B), F32)],
        ),
        out_shape=jax.ShapeDtypeStruct(start.shape, F32),
        compiler_params=pltpu.CompilerParams(vmem_limit_bytes=56 << 20),
        cost_estimate=pl.CostEstimate(flops=3 << 31, bytes_accessed=14 << 20, transcendentals=0),
        name="last_sums",
    )(at[None], hi, hi, lo, lo, *far, start)


def rows_of(core, a, kept, came):
    parts = []
    for x in range(2):
        k, c = kept[x, core, a // 2, a % 2], came[x, core, a // 2, a % 2]
        parts += [jnp.where(core == 0, k, c), jnp.where(core == 0, c, k)]
    return jnp.concatenate(parts, axis=0)


def share_kernel(where, picks, u_ref, kept, came, out_ref, total):
    total[...] = jnp.zeros_like(total)
    for a in range(16):
        pick = picks[a]

        @pl.when(pick >= 0)
        def _(a=a, pick=pick):
            total[...] += dot3(rows_of(where[0], a, kept, came), u_ref[jnp.maximum(pick, 0)])

    out_ref[...] = total[...].T


def panel_kernel(where, picks, kept, came, panel_ref):
    for a in range(16):
        panel_ref[a] = jnp.where(picks[a] >= 0, -rows_of(where[0], a, kept, came).T, 0.0)


def on_one(kernel, name, core, picks, arrays, shape, scratch=(), flops=0):
    full = lambda s: pl.BlockSpec(s, lambda i, w, p: (0,) * len(s))
    return pl.pallas_call(
        kernel,
        grid_spec=pltpu.PrefetchScalarGridSpec(
            num_scalar_prefetch=2,
            grid=(1,),
            in_specs=[full(t.shape) for t in arrays],
            out_specs=full(shape),
            scratch_shapes=scratch,
        ),
        out_shape=jax.ShapeDtypeStruct(shape, F32),
        compiler_params=pltpu.CompilerParams(vmem_limit_bytes=16 << 20),
        cost_estimate=pl.CostEstimate(flops=flops, bytes_accessed=4 << 20, transcendentals=0),
        name=name,
    )(core[None], picks, *arrays)


def after(x, *earlier):
    return lax.optimization_barrier((x, *earlier))[0]


def gather(sigma, first, second):
    sigma, first, second = lax.optimization_barrier((sigma, first, second))
    x1 = swap(sigma, X1, X3)
    a = jnp.stack([first, *ring(first, Z1, Z3)])
    b = jnp.stack([second, *ring(second, Y1, Y3)])
    sigma, x1, a, b = lax.optimization_barrier((sigma, x1, a, b))
    x2 = swap(sigma, X3, X1)
    a2, b2 = swap(a, Y3, Y1), swap(b, Z3, Z1)
    a1, b1 = swap(after(a, a2), Y1, Y3), swap(after(b, b2), Z1, Z3)
    a3, b3 = swap(a2, Y1, Y3), swap(b2, Z1, Z3)
    sigma_other, x1_other = swap(sigma, CORE), swap(x1, CORE)
    x3 = swap(after(x2, a2, b2, sigma_other, x1_other), X1, X3)
    sigmas = (x1, swap(x2, CORE), x2, x1_other, sigma, sigma_other)
    return sigmas, (x3, swap(x3, CORE)), (a, a1, a2, a3, b, b1, b2, b3)


def local(sigma_anc, panel_u, structure, diag_inv):
    col, row = lax.axis_index("col"), lax.axis_index("row")
    x_hi, z, y = col // 16, (col // 4) % 4, col % 4
    x_lo, core = row // 2, row % 2
    panel = panel_u[0]

    sigmas, far, pieces = gather(sigma_anc, *cut(panel, structure, row))

    away = jnp.stack([0 * core, 1 + 2 * core, 3 - 2 * core, 2 + 0 * core]).astype(jnp.int32)
    there_z, there_y = z ^ away, y ^ away
    nodes = jnp.stack([there_y[:, None] + there_z * 4, there_z[:, None] * 4 + there_y]).reshape(-1)
    entry = jnp.arange(32, dtype=jnp.int32)
    mine = jnp.sum(jnp.where(structure[0][:, None] == (16 * row + jnp.arange(16))[None, :], entry[:, None] + 1, 0), axis=0) - 1

    base = lambda x: [32 * x + 16 * core, 32 * x + 16 * (1 - core)]
    where = jnp.stack(base(1 - x_lo) + base(x_lo) + [x_hi ^ core, x_hi])
    part, hi, lo = first_sums(nodes, where, pieces, sigmas)
    part = last_sums(1 - x_hi, hi, lo, far, part)
    groups = [
        [h * 64 + q * 4 + l * 2 + c for l in range(2) for q in range(16)] for h in range(2) for c in range(2)
    ]
    moved = lax.all_to_all(part.reshape(32, 2, Q, B), AXES, 0, 0, axis_index_groups=groups, tiled=True)
    parts = [t.reshape(2, 2, 8, 2, Q, B) for t in (moved, swap(moved, CORE))]
    share = on_one(share_kernel, "share", core, mine, [panel, *parts], (B, B), [pltpu.VMEM((B, B), F32)], 1 << 27)

    square = jnp.einsum("zx,zy->xy", diag_inv[0], diag_inv[0], precision=lax.Precision.HIGHEST)
    others = [swap(share, mask) for mask in (CORE, X1, X1 + CORE)]
    panel_out = on_one(panel_kernel, "panel", core, mine, parts, (16, B, B))
    diag = square + share + (others[0] + (others[1] + others[2]))
    return panel_out[None], diag[None]


def solution(mesh):
    return jax.shard_map(
        local,
        mesh=mesh,
        in_specs=(P("row", "col", None, None), P("col", None, None, None), P("col", None), P("col", None, None)),
        out_specs=(P("col", "row", None, None), P("col", None, None)),
        check_vma=False,
    )
```

```python
import functools

import jax
import jax.numpy as jnp
from jax import lax
from jax.experimental import pallas as pl
from jax.experimental.pallas import tpu as pltpu
from jax.sharding import PartitionSpec as P

AXES = ("col", "row")
CORE = 1
X1, X3 = 2, 66
Y1, Y3 = 4, 12
Z1, Z3 = 16, 48
B = 128
Q = 32
F32, BF16 = jnp.float32, jnp.bfloat16
MANY = 4


def swap(x, even, odd=None):
    odd = even if odd is None else odd
    return lax.ppermute(x, AXES, [(i, i ^ (odd if i % 2 else even)) for i in range(128)])


def ring(x, one, three):
    first = swap(x, one, three)
    second = swap(x, three, one)
    return first, second, swap(second, one, three)


def split(x):
    hi = x.astype(BF16)
    return hi, (x - hi.astype(F32)).astype(BF16)


def dot(a, b):
    return jnp.dot(a, b, preferred_element_type=F32)


def dot3(a, b):
    (ah, al), (bh, bl) = split(a), split(b)
    return dot(ah, bh) + (dot(ah, bl) + dot(al, bh))


def cut_kernel(where, u_ref, label_ref, first_ref, second_ref, turned):
    half = u_ref.shape[0] // 2

    def step(k, carry):
        for i, out_ref in enumerate((first_ref, second_ref)):
            turned[i] = u_ref[i * half + k].T
            out_ref[k] = turned[i, pl.ds(pl.multiple_of(where[0] * Q, Q), Q), :]
        return carry

    lax.fori_loop(0, half, step, 0, unroll=4)
    for out_ref in (first_ref, second_ref):
        out_ref[half] = jnp.zeros_like(out_ref[half])
        out_ref[half, :, :32] = jnp.broadcast_to(label_ref[...].astype(F32), (Q, 32))


def cut(panel, labels, row):
    return pl.pallas_call(
        cut_kernel,
        grid_spec=pltpu.PrefetchScalarGridSpec(
            num_scalar_prefetch=1,
            grid=(1,),
            in_specs=[
                pl.BlockSpec((32, B, B), lambda i, w: (0, 0, 0)),
                pl.BlockSpec((1, 32), lambda i, w: (0, 0)),
            ],
            out_specs=[pl.BlockSpec((17, Q, B), lambda i, w: (0, 0, 0))] * 2,
            scratch_shapes=[pltpu.VMEM((2, B, B), F32)],
        ),
        out_shape=[jax.ShapeDtypeStruct((17, Q, B), F32)] * 2,
        name="cut",
    )(row[None], panel, labels)


ON_CHIP = pl.BlockSpec(memory_space=pltpu.VMEM)
SCALARS = pl.BlockSpec(memory_space=pltpu.SMEM)


def gained(weights, blocks, sides):
    tall = [
        jnp.concatenate([blocks[side][core][i, low] for side in range(sides) for low in range(2)], axis=1)
        for core in range(2)
        for i in range(MANY)
    ]
    high, low = split(jnp.concatenate(tall, axis=0))
    wh, wl = (jnp.concatenate(t, axis=1) for t in weights)
    return dot(wh, high) + (dot(wh, low) + dot(wl, high))


def sums_kernel(halves, more, nodes, where, *refs):
    count = len(halves)
    given, refs = refs[: count + 6 + 3 * more], refs[count + 6 + 3 * more :]
    (out_ref, hi_out, lo_out), refs = refs[:3], refs[3:]
    hi_ref, lo_ref, w, held, total, labels, landed, arrived, left, read, *own = refs
    parts = [pltpu.make_async_copy(t, w.at[i], landed.at[i]) for i, t in enumerate(given[:count])]
    texts = [
        pltpu.make_async_copy(t.at[:, 16, pl.ds(0, 8)], labels.at[i], read.at[i]) for i, t in enumerate(given[:count])
    ]
    copies = [pltpu.make_async_copy(t, held.at[i], arrived.at[i]) for i, t in enumerate(given[count : count + 6])]
    inward = []
    if more:
        out_ref[...] = given[-1][...]
        merged, filled = own
        inward = [
            pltpu.make_async_copy(t, merged.at[i, pl.ds(0, 32)], filled.at[i])
            for i, t in enumerate(given[count + 6 : count + 8])
        ]
    for copy in texts + parts + copies + inward:
        copy.start()

    def clear(b, carry):
        hi_ref[b] = jnp.zeros_like(hi_ref[b])
        lo_ref[b] = jnp.zeros_like(lo_ref[b])
        return carry

    lax.fori_loop(0, hi_ref.shape[0], clear, 0)
    for copy in texts:
        copy.wait()

    def put(i, row_of, place_of, hi_to, lo_to):
        def node(n, carry):
            rows = pl.ds(pl.multiple_of(row_of(n), Q), Q)
            for k in range(16):
                at = place_of(labels[i, n, 0, halves[i] * 16 + k].astype(jnp.int32))
                hi, lo = split(w[i, n, k])
                hi_to[at, rows, :] = hi
                lo_to[at, rows, :] = lo
            return carry

        lax.fori_loop(0, 4, node, 0)

    for i, part in enumerate(parts):
        part.wait()
        put(i, lambda n: (i * 4 + n if more else nodes[i * 4 + n]) * Q, lambda at: at, hi_ref, lo_ref)
    for copy in copies:
        copy.wait()

    def run(first, sides, blocks):
        total[:, : 2 * sides * B] = jnp.zeros((total.shape[0], 2 * sides * B), F32)

        def step(t, carry):
            k = pl.multiple_of(t * MANY, MANY)
            weights = [
                [ref[where[first + core] + k + i] for core in range(2) for i in range(MANY)] for ref in (hi_ref, lo_ref)
            ]
            here = [[held.at[i, pl.ds(k, MANY)] for i in side] for side in blocks]
            total[:, : 2 * sides * B] += gained(weights, here, sides)
            return carry

        lax.fori_loop(0, 16 // MANY, step, 0)

    def add(at, columns, fresh):
        for n in range(columns):
            place, column = at ^ (n // 2), total.at[:, n * B : (n + 1) * B]
            if more:
                for i in range(4 * count):
                    out_ref[place, nodes[i], n % 2] += column[i * Q : (i + 1) * Q]
            elif fresh:
                out_ref[place, :, n % 2] = column[...].reshape(16, Q, B)
            else:
                out_ref[place, :, n % 2] += column[...].reshape(16, Q, B)

    run(0, 2, [(0, 1), (2, 3)])
    add(where[4], 4, True)
    half = where[6]
    sources = [ref.at[pl.ds(half, 32)] for ref in (hi_ref, lo_ref)]
    if more:
        for copy in inward:
            copy.wait()
        inside = lambda at: jnp.where(jnp.logical_and(at >= half, at < half + 32), at - half, 32)
        for i in range(count):
            put(i, lambda n: nodes[i * 4 + n] * Q, inside, merged.at[0], merged.at[1])
        sources = [merged.at[i, pl.ds(0, 32)] for i in range(2)]
    outward = [
        pltpu.make_async_copy(source, out, left.at[i]) for i, (source, out) in enumerate(zip(sources, (hi_out, lo_out)))
    ]
    for copy in outward:
        copy.start()
    run(2, 1, [(4, 5)])
    add(where[5], 2, False)
    for copy in outward:
        copy.wait()


def sums(nodes, where, parts, halves, sigmas, earlier=()):
    whole, count, more = pl.BlockSpec(memory_space=pl.ANY), len(parts), len(earlier) > 0
    rows = count * 4 * Q if more else 16 * Q
    return pl.pallas_call(
        functools.partial(sums_kernel, halves, more),
        in_specs=[SCALARS] * 2 + [whole] * (count + 6 + 2 * more) + [ON_CHIP] * more,
        out_specs=[ON_CHIP, whole, whole],
        out_shape=[jax.ShapeDtypeStruct((2, 16, 2, Q, B), F32)] + [jax.ShapeDtypeStruct((32, 16 * Q, B), BF16)] * 2,
        scratch_shapes=[
            pltpu.VMEM((64, rows, B), BF16),
            pltpu.VMEM((64, rows, B), BF16),
            pltpu.VMEM((count, 4, 17, Q, B), F32),
            pltpu.VMEM((6, 16, 2, B, B), F32),
            pltpu.VMEM((rows, 4 * B), F32),
            pltpu.SMEM((count, 4, 8, B), F32),
            pltpu.SemaphoreType.DMA((count,)),
            pltpu.SemaphoreType.DMA((6,)),
            pltpu.SemaphoreType.DMA((2,)),
            pltpu.SemaphoreType.DMA((count,)),
        ]
        + [pltpu.VMEM((2, 33, 16 * Q, B), BF16), pltpu.SemaphoreType.DMA((2,))] * more,
        compiler_params=pltpu.CompilerParams(vmem_limit_bytes=48 << 20),
        cost_estimate=pl.CostEstimate(flops=9 << 31, bytes_accessed=32 << 20, transcendentals=0),
        name="sums_of_more" if more else "sums",
    )(nodes, where, *parts, *sigmas, *earlier)


def last_kernel(where, hi, lo, far0, far1, start, out_ref, weights, held, total, arrived):
    at, steps = where[0], 16 // MANY
    copies = []
    for t in range(steps):
        block = lambda first: pl.ds(first + t * MANY, MANY)
        pairs = [(ref.at[block(16 * (core ^ where[1]))], weights.at[i, block(16 * core)]) for i, ref in enumerate((hi, lo)) for core in range(2)]
        pairs += [(ref.at[block(0)], held.at[core, block(0)]) for core, ref in enumerate((far0, far1))]
        copies.append([pltpu.make_async_copy(*pair, arrived.at[t, i]) for i, pair in enumerate(pairs)])
        for copy in copies[-1]:
            copy.start()
    out_ref[1 - at] = start[1 - at]
    for n in range(2):
        total[:, n * B : (n + 1) * B] = start[at, :, n].reshape(16 * Q, B)
    for t in range(steps):
        for copy in copies[t]:
            copy.wait()
        each = range(t * MANY, (t + 1) * MANY)
        w = [[weights[i, 16 * core + k] for core in range(2) for k in each] for i in range(2)]
        total[...] += gained(w, [[held.at[core, pl.ds(t * MANY, MANY)] for core in range(2)]], 1)
    for n in range(2):
        out_ref[at, :, n] = total[:, n * B : (n + 1) * B].reshape(16, Q, B)


def last_sums(at, hi, lo, far, start):
    rows, away = 16 * Q, pl.BlockSpec(memory_space=pl.ANY)
    return pl.pallas_call(
        last_kernel,
        in_specs=[SCALARS] + [away] * 4 + [ON_CHIP],
        out_specs=ON_CHIP,
        scratch_shapes=[
            pltpu.VMEM((2, 32, rows, B), BF16),
            pltpu.VMEM((2, 16, 2, B, B), F32),
            pltpu.VMEM((rows, 2 * B), F32),
            pltpu.SemaphoreType.DMA((16 // MANY, 6)),
        ],
        out_shape=jax.ShapeDtypeStruct(start.shape, F32),
        compiler_params=pltpu.CompilerParams(vmem_limit_bytes=56 << 20),
        cost_estimate=pl.CostEstimate(flops=3 << 31, bytes_accessed=14 << 20, transcendentals=0),
        name="last_sums",
    )(at, hi, lo, *far, start)


def rows_of(core, a, kept, came):
    parts = []
    for x in range(2):
        k, c = kept[x, core, a // 2, a % 2], came[x, core, a // 2, a % 2]
        parts += [jnp.where(core == 0, k, c), jnp.where(core == 0, c, k)]
    return jnp.concatenate(parts, axis=0)


def share_kernel(where, picks, u_ref, kept, came, out_ref, total):
    total[...] = jnp.zeros_like(total)
    for a in range(16):
        pick = picks[a]

        @pl.when(pick >= 0)
        def _(a=a, pick=pick):
            total[...] += dot3(rows_of(where[0], a, kept, came), u_ref[jnp.maximum(pick, 0)])

    out_ref[...] = total[...].T


def panel_kernel(where, picks, kept, came, panel_ref):
    for a in range(16):
        panel_ref[a] = jnp.where(picks[a] >= 0, -rows_of(where[0], a, kept, came).T, 0.0)


def on_one(kernel, name, core, picks, arrays, shape, scratch=(), flops=0):
    full = lambda s: pl.BlockSpec(s, lambda i, w, p: (0,) * len(s))
    return pl.pallas_call(
        kernel,
        grid_spec=pltpu.PrefetchScalarGridSpec(
            num_scalar_prefetch=2,
            grid=(1,),
            in_specs=[full(t.shape) for t in arrays],
            out_specs=full(shape),
            scratch_shapes=scratch,
        ),
        out_shape=jax.ShapeDtypeStruct(shape, F32),
        compiler_params=pltpu.CompilerParams(vmem_limit_bytes=16 << 20),
        cost_estimate=pl.CostEstimate(flops=flops, bytes_accessed=4 << 20, transcendentals=0),
        name=name,
    )(core[None], picks, *arrays)


def after(x, *earlier):
    return lax.optimization_barrier((x, *earlier))[0]


def gather(sigma, first, second):
    sigma, first, second = lax.optimization_barrier((sigma, first, second))
    x1 = swap(sigma, X1, X3)
    a = jnp.stack([first, *ring(first, Z1, Z3)])
    b = jnp.stack([second, *ring(second, Y1, Y3)])
    other = lambda t: swap(t, CORE)
    sigma, x1, a, b, sigma_other = lax.optimization_barrier((sigma, x1, a, b, other(sigma)))
    x2 = swap(sigma, X3, X1)
    a2, b2 = swap(a, Y3, Y1), swap(b, Z3, Z1)
    a1, b1 = swap(a, Y1, Y3), swap(b, Z1, Z3)
    x2, a1, a2, b1, b2 = lax.optimization_barrier((x2, a1, a2, b1, b2))
    x3 = swap(x2, X1, X3)
    a3, b3 = swap(a2, Y1, Y3), swap(b2, Z1, Z3)
    sigmas = (x1, other(x2), x2, other(x1), sigma, sigma_other)
    return sigmas, x3, (a, a1, a2, b, b1, b2), (a3, b3)


def local(sigma_anc, panel_u, structure, diag_inv):
    col, row = lax.axis_index("col"), lax.axis_index("row")
    x_hi, z, y = col // 16, (col // 4) % 4, col % 4
    x_lo, core = row // 2, row % 2
    panel = panel_u[0]

    sigmas, far, most, rest = gather(sigma_anc, *cut(panel, structure, row))

    away = jnp.stack([0 * core, 1 + 2 * core, 3 - 2 * core, 2 + 0 * core]).astype(jnp.int32)
    there_z, there_y = z ^ away, y ^ away
    nodes = jnp.stack([there_y[:, None] + there_z * 4, there_z[:, None] * 4 + there_y])
    entry = jnp.arange(32, dtype=jnp.int32)
    mine = jnp.sum(jnp.where(structure[0][:, None] == (16 * row + jnp.arange(16))[None, :], entry[:, None] + 1, 0), axis=0) - 1

    base = lambda x: [32 * x + 16 * core, 32 * x + 16 * (1 - core)]
    where = jnp.stack(base(1 - x_lo) + base(x_lo) + [x_hi ^ core, x_hi, 32 * x_lo])
    part, hi, lo = sums(nodes[:, :3].reshape(-1), where, most, (0, 0, 0, 1, 1, 1), sigmas)
    far = after(far, part)
    far = (far, swap(far, CORE))
    part, hi, lo = sums(nodes[:, 3].reshape(-1), where, rest, (0, 1), sigmas, (hi, lo, part))
    part = last_sums(jnp.stack([1 - x_hi, core]), hi, lo, far, part)
    groups = [
        [h * 64 + q * 4 + l * 2 + c for l in range(2) for q in range(16)] for h in range(2) for c in range(2)
    ]
    moved = lax.all_to_all(part.reshape(32, 2, Q, B), AXES, 0, 0, axis_index_groups=groups, tiled=True)
    parts = [t.reshape(2, 2, 8, 2, Q, B) for t in (moved, swap(moved, CORE))]
    share = on_one(share_kernel, "share", core, mine, [panel, *parts], (B, B), [pltpu.VMEM((B, B), F32)], 1 << 27)

    square = jnp.einsum("zx,zy->xy", diag_inv[0], diag_inv[0], precision=lax.Precision.HIGHEST)
    others = [swap(share, mask) for mask in (CORE, X1, X1 + CORE)]
    panel_out = on_one(panel_kernel, "panel", core, mine, parts, (16, B, B))
    diag = square + share + (others[0] + (others[1] + others[2]))
    return panel_out[None], diag[None]


def solution(mesh):
    return jax.shard_map(
        local,
        mesh=mesh,
        in_specs=(P("row", "col", None, None), P("col", None, None, None), P("col", None), P("col", None, None)),
        out_specs=(P("col", "row", None, None), P("col", None, None)),
        check_vma=False,
    )
```

```python
import functools

import jax
import jax.numpy as jnp
from jax import lax
from jax.experimental import pallas as pl
from jax.experimental.pallas import tpu as pltpu
from jax.sharding import PartitionSpec as P

AXES = ("col", "row")
CORE = 1
X1, X3 = 2, 66
Y1, Y3 = 4, 12
Z1, Z3 = 16, 48
B = 128
Q = 32
F32, BF16 = jnp.float32, jnp.bfloat16
MANY = 4


def swap(x, even, odd=None):
    odd = even if odd is None else odd
    return lax.ppermute(x, AXES, [(i, i ^ (odd if i % 2 else even)) for i in range(128)])


def ring(x, one, three):
    first = swap(x, one, three)
    second = swap(x, three, one)
    return first, second, swap(second, one, three)


def split(x):
    hi = x.astype(BF16)
    return hi, (x - hi.astype(F32)).astype(BF16)


def dot(a, b):
    return jnp.dot(a, b, preferred_element_type=F32)


def dot3(a, b):
    (ah, al), (bh, bl) = split(a), split(b)
    return dot(ah, bh) + (dot(ah, bl) + dot(al, bh))


def cut_kernel(where, u_ref, label_ref, first_ref, second_ref, turned):
    half = u_ref.shape[0] // 2

    def step(k, carry):
        for i, out_ref in enumerate((first_ref, second_ref)):
            turned[i] = u_ref[i * half + k].T
            out_ref[k] = turned[i, pl.ds(pl.multiple_of(where[0] * Q, Q), Q), :]
        return carry

    lax.fori_loop(0, half, step, 0, unroll=4)
    for out_ref in (first_ref, second_ref):
        out_ref[half] = jnp.zeros_like(out_ref[half])
        out_ref[half, :, :32] = jnp.broadcast_to(label_ref[...].astype(F32), (Q, 32))


def cut(panel, labels, row):
    return pl.pallas_call(
        cut_kernel,
        grid_spec=pltpu.PrefetchScalarGridSpec(
            num_scalar_prefetch=1,
            grid=(1,),
            in_specs=[
                pl.BlockSpec((32, B, B), lambda i, w: (0, 0, 0)),
                pl.BlockSpec((1, 32), lambda i, w: (0, 0)),
            ],
            out_specs=[pl.BlockSpec((17, Q, B), lambda i, w: (0, 0, 0))] * 2,
            scratch_shapes=[pltpu.VMEM((2, B, B), F32)],
        ),
        out_shape=[jax.ShapeDtypeStruct((17, Q, B), F32)] * 2,
        name="cut",
    )(row[None], panel, labels)


ON_CHIP = pl.BlockSpec(memory_space=pltpu.VMEM)
SCALARS = pl.BlockSpec(memory_space=pltpu.SMEM)


def gained(weights, blocks, sides):
    tall = [
        jnp.concatenate([blocks[side][core][i, low] for side in range(sides) for low in range(2)], axis=1)
        for core in range(2)
        for i in range(MANY)
    ]
    high, low = split(jnp.concatenate(tall, axis=0))
    wh, wl = (jnp.concatenate(t, axis=1) for t in weights)
    return dot(wh, high) + (dot(wh, low) + dot(wl, high))


def first_kernel(nodes, where, *refs):
    out_ref, hi_out, lo_out, hi_ref, lo_ref, w, held, total, labels, landed, arrived, left, read = refs[14:]
    parts = [pltpu.make_async_copy(t, w.at[i], landed.at[i]) for i, t in enumerate(refs[:8])]
    sigmas = refs[8:14]
    texts = [
        pltpu.make_async_copy(t.at[:, 16, pl.ds(0, 8)], labels.at[i], read.at[i]) for i, t in enumerate(refs[:8])
    ]
    for copy in texts + parts:
        copy.start()
    copies = [pltpu.make_async_copy(t, held.at[i], arrived.at[i]) for i, t in enumerate(sigmas)]
    for copy in copies:
        copy.start()

    def clear(b, carry):
        hi_ref[b] = jnp.zeros_like(hi_ref[b])
        lo_ref[b] = jnp.zeros_like(lo_ref[b])
        return carry

    lax.fori_loop(0, hi_ref.shape[0], clear, 0)
    for copy in texts:
        copy.wait()
    for i, part in enumerate(parts):
        part.wait()

        def node(n, carry, i=i):
            rows = pl.ds(pl.multiple_of(nodes[i * 4 + n] * Q, Q), Q)
            for k in range(16):
                at = labels[i, n, 0, i // 4 * 16 + k].astype(jnp.int32)
                hi, lo = split(w[i, n, k])
                hi_ref[at, rows, :] = hi
                lo_ref[at, rows, :] = lo
            return carry

        lax.fori_loop(0, 4, node, 0)

    outward = [
        pltpu.make_async_copy(ref.at[pl.ds(where[2 + core], 16)], out.at[pl.ds(16 * core, 16)], left.at[2 * i + core])
        for i, (ref, out) in enumerate(((hi_ref, hi_out), (lo_ref, lo_out)))
        for core in range(2)
    ]
    for copy in outward:
        copy.start()
    for copy in copies:
        copy.wait()

    def run(first, sides, blocks):
        def step(t, carry):
            k = pl.multiple_of(t * MANY, MANY)
            weights = [
                [ref[where[first + core] + k + i] for core in range(2) for i in range(MANY)] for ref in (hi_ref, lo_ref)
            ]
            here = [[held.at[i, pl.ds(k, MANY)] for i in side] for side in blocks]
            total[:, : 2 * sides * B] += gained(weights, here, sides)
            return carry

        lax.fori_loop(0, 16 // MANY, step, 0)

    total[...] = jnp.zeros_like(total)
    run(0, 2, [(0, 1), (2, 3)])
    at = where[4]
    for n in range(4):
        out_ref[at ^ (n // 2), :, n % 2] = total[:, n * B : (n + 1) * B].reshape(16, Q, B)
    total[...] = jnp.zeros_like(total)
    run(2, 1, [(4, 5)])
    for n in range(2):
        out_ref[where[5], :, n] += total[:, n * B : (n + 1) * B].reshape(16, Q, B)
    for copy in outward:
        copy.wait()


def first_sums(nodes, where, parts, sigmas):
    whole = pl.BlockSpec(memory_space=pl.ANY)
    rows = 16 * Q
    return pl.pallas_call(
        first_kernel,
        in_specs=[SCALARS] * 2 + [whole] * 14,
        out_specs=[ON_CHIP, whole, whole],
        out_shape=[jax.ShapeDtypeStruct((2, 16, 2, Q, B), F32)] + [jax.ShapeDtypeStruct((32, rows, B), BF16)] * 2,
        scratch_shapes=[
            pltpu.VMEM((64, rows, B), BF16),
            pltpu.VMEM((64, rows, B), BF16),
            pltpu.VMEM((8, 4, 17, Q, B), F32),
            pltpu.VMEM((6, 16, 2, B, B), F32),
            pltpu.VMEM((rows, 4 * B), F32),
            pltpu.SMEM((8, 4, 8, B), F32),
            pltpu.SemaphoreType.DMA((8,)),
            pltpu.SemaphoreType.DMA((6,)),
            pltpu.SemaphoreType.DMA((4,)),
            pltpu.SemaphoreType.DMA((8,)),
        ],
        compiler_params=pltpu.CompilerParams(vmem_limit_bytes=48 << 20),
        cost_estimate=pl.CostEstimate(flops=9 << 31, bytes_accessed=32 << 20, transcendentals=0),
        name="first_sums",
    )(nodes, where, *parts, *sigmas)


def last_kernel(where, hi, lo, far0, far1, start, out_ref, weights, held, total, arrived):
    at, steps = where[0], 16 // MANY
    copies = []
    for t in range(steps):
        block = lambda first: pl.ds(first + t * MANY, MANY)
        pairs = [(ref.at[block(16 * core)], weights.at[i, block(16 * core)]) for i, ref in enumerate((hi, lo)) for core in range(2)]
        pairs += [(ref.at[block(0)], held.at[core, block(0)]) for core, ref in enumerate((far0, far1))]
        copies.append([pltpu.make_async_copy(*pair, arrived.at[t, i]) for i, pair in enumerate(pairs)])
        for copy in copies[-1]:
            copy.start()
    out_ref[1 - at] = start[1 - at]
    for n in range(2):
        total[:, n * B : (n + 1) * B] = start[at, :, n].reshape(16 * Q, B)
    for t in range(steps):
        for copy in copies[t]:
            copy.wait()
        each = range(t * MANY, (t + 1) * MANY)
        w = [[weights[i, 16 * core + k] for core in range(2) for k in each] for i in range(2)]
        total[...] += gained(w, [[held.at[core, pl.ds(t * MANY, MANY)] for core in range(2)]], 1)
    for n in range(2):
        out_ref[at, :, n] = total[:, n * B : (n + 1) * B].reshape(16, Q, B)


def last_sums(at, hi, lo, far, start):
    rows, away = 16 * Q, pl.BlockSpec(memory_space=pl.ANY)
    return pl.pallas_call(
        last_kernel,
        in_specs=[SCALARS] + [away] * 4 + [ON_CHIP],
        out_specs=ON_CHIP,
        scratch_shapes=[
            pltpu.VMEM((2, 32, rows, B), BF16),
            pltpu.VMEM((2, 16, 2, B, B), F32),
            pltpu.VMEM((rows, 2 * B), F32),
            pltpu.SemaphoreType.DMA((16 // MANY, 6)),
        ],
        out_shape=jax.ShapeDtypeStruct(start.shape, F32),
        compiler_params=pltpu.CompilerParams(vmem_limit_bytes=56 << 20),
        cost_estimate=pl.CostEstimate(flops=3 << 31, bytes_accessed=14 << 20, transcendentals=0),
        name="last_sums",
    )(at[None], hi, lo, *far, start)


def rows_of(core, a, kept, came):
    parts = []
    for x in range(2):
        k, c = kept[x, core, a // 2, a % 2], came[x, core, a // 2, a % 2]
        parts += [jnp.where(core == 0, k, c), jnp.where(core == 0, c, k)]
    return jnp.concatenate(parts, axis=0)


def share_kernel(where, picks, u_ref, kept, came, out_ref, total):
    total[...] = jnp.zeros_like(total)
    for a in range(16):
        pick = picks[a]

        @pl.when(pick >= 0)
        def _(a=a, pick=pick):
            total[...] += dot3(rows_of(where[0], a, kept, came), u_ref[jnp.maximum(pick, 0)])

    out_ref[...] = total[...].T


def panel_kernel(where, picks, kept, came, panel_ref):
    for a in range(16):
        panel_ref[a] = jnp.where(picks[a] >= 0, -rows_of(where[0], a, kept, came).T, 0.0)


def on_one(kernel, name, core, picks, arrays, shape, scratch=(), flops=0):
    full = lambda s: pl.BlockSpec(s, lambda i, w, p: (0,) * len(s))
    return pl.pallas_call(
        kernel,
        grid_spec=pltpu.PrefetchScalarGridSpec(
            num_scalar_prefetch=2,
            grid=(1,),
            in_specs=[full(t.shape) for t in arrays],
            out_specs=full(shape),
            scratch_shapes=scratch,
        ),
        out_shape=jax.ShapeDtypeStruct(shape, F32),
        compiler_params=pltpu.CompilerParams(vmem_limit_bytes=16 << 20),
        cost_estimate=pl.CostEstimate(flops=flops, bytes_accessed=4 << 20, transcendentals=0),
        name=name,
    )(core[None], picks, *arrays)


def after(x, *earlier):
    return lax.optimization_barrier((x, *earlier))[0]


def gather(sigma, first, second):
    sigma, first, second = lax.optimization_barrier((sigma, first, second))
    x1 = swap(sigma, X1, X3)
    a = jnp.stack([first, *ring(first, Z1, Z3)])
    b = jnp.stack([second, *ring(second, Y1, Y3)])
    other = lambda t: swap(t, CORE)
    sigma, x1, a, b, sigma_other = lax.optimization_barrier((sigma, x1, a, b, other(sigma)))
    x2 = swap(sigma, X3, X1)
    a2, b2 = swap(a, Y3, Y1), swap(b, Z3, Z1)
    a1, b1 = swap(a, Y1, Y3), swap(b, Z1, Z3)
    x2, a1, a2, b1, b2 = lax.optimization_barrier((x2, a1, a2, b1, b2))
    x3 = swap(x2, X1, X3)
    a3, b3 = swap(a2, Y1, Y3), swap(b2, Z1, Z3)
    sigmas = (x1, other(x2), x2, other(x1), sigma, sigma_other)
    return sigmas, x3, (a, a1, a2, a3, b, b1, b2, b3)


def local(sigma_anc, panel_u, structure, diag_inv):
    col, row = lax.axis_index("col"), lax.axis_index("row")
    x_hi, z, y = col // 16, (col // 4) % 4, col % 4
    x_lo, core = row // 2, row % 2
    panel = panel_u[0]

    sigmas, far, pieces = gather(sigma_anc, *cut(panel, structure, row))

    away = jnp.stack([0 * core, 1 + 2 * core, 3 - 2 * core, 2 + 0 * core]).astype(jnp.int32)
    there_z, there_y = z ^ away, y ^ away
    nodes = jnp.stack([there_y[:, None] + there_z * 4, there_z[:, None] * 4 + there_y]).reshape(-1)
    entry = jnp.arange(32, dtype=jnp.int32)
    mine = jnp.sum(jnp.where(structure[0][:, None] == (16 * row + jnp.arange(16))[None, :], entry[:, None] + 1, 0), axis=0) - 1

    base = lambda x: [32 * x + 16 * core, 32 * x + 16 * (1 - core)]
    where = jnp.stack(base(1 - x_lo) + base(x_lo) + [x_hi ^ core, x_hi])
    part, hi, lo = first_sums(nodes, where, pieces, sigmas)
    far = after(far, part)
    part = last_sums(1 - x_hi, hi, lo, (far, swap(far, CORE)), part)
    groups = [
        [h * 64 + q * 4 + l * 2 + c for l in range(2) for q in range(16)] for h in range(2) for c in range(2)
    ]
    moved = lax.all_to_all(part.reshape(32, 2, Q, B), AXES, 0, 0, axis_index_groups=groups, tiled=True)
    parts = [t.reshape(2, 2, 8, 2, Q, B) for t in (moved, swap(moved, CORE))]
    share = on_one(share_kernel, "share", core, mine, [panel, *parts], (B, B), [pltpu.VMEM((B, B), F32)], 1 << 27)

    square = jnp.einsum("zx,zy->xy", diag_inv[0], diag_inv[0], precision=lax.Precision.HIGHEST)
    others = [swap(share, mask) for mask in (CORE, X1, X1 + CORE)]
    panel_out = on_one(panel_kernel, "panel", core, mine, parts, (16, B, B))
    diag = square + share + (others[0] + (others[1] + others[2]))
    return panel_out[None], diag[None]


def solution(mesh):
    return jax.shard_map(
        local,
        mesh=mesh,
        in_specs=(P("row", "col", None, None), P("col", None, None, None), P("col", None), P("col", None, None)),
        out_specs=(P("col", "row", None, None), P("col", None, None)),
        check_vma=False,
    )
```
